512 devices in a mesh: ctx: 32 (over y, x), tp: 16 (over z, core).
Axes of the slice: x: 4, y: 8, z: 8, core: 2. Of those that a mesh axis runs over, the one named last changes fastest.
Arguments:
- query_states: bfloat16 [8192, 8192], P('ctx', 'tp'), may hold values from -250 to 250
- key_matrix: bfloat16 [8192, 1024], P('ctx'), may hold values from -8 to 8
- value_matrix: bfloat16 [8192, 1024], P('ctx'), may hold values from -6 to 6
- hidden: bfloat16 [8192, 14336], P('ctx', 'tp'), may hold values from -6 to 6
- down_weight: bfloat16 [14336, 8192], P('tp', 'ctx'), may hold values from -0.046875 to 0.046875
- out_weight: bfloat16 [8192, 8192], P('tp', 'ctx'), may hold values from -0.0625 to 0.0625
- encoder: bfloat16 [8192, 1024], P('ctx'), may hold values from -0.0625 to 0.0625
- decoder: bfloat16 [1024, 8192], P(None, 'tp'), may hold values from -0.1875 to 0.1875
- cotangent: bfloat16 [8192, 8192], P('ctx', 'tp'), may hold values from -6 to 6
Outputs:
- attended: bfloat16 [8192, 8192], P('ctx', 'tp')
- decoded: bfloat16 [8192, 8192], P('ctx', 'tp')
- grad_hidden: bfloat16 [8192, 14336], P('ctx', 'tp')
- grad_attended: bfloat16 [8192, 8192], P('ctx', 'tp')
The draws below stay inside these ranges and needn't reach their ends.
All inputs are finite; a program needn't handle non-finite values.
Results may differ from the reference program's by a relative error of at most 0.035.
Values may be sent and summed in bfloat16 or wider, within the bound.
A program may use at most 64 MiB of HBM per device.

```python
import math
import jax
import jax.numpy as jnp
from jax import lax

D = 8192
HEAD_WIDTH = 128
HQ_DEV = 4
QUERY_PER_KEY = 8
FF_DEV = 896
R = 1024
TOKEN_COUNT = 8192
QUERY_HEADS = 64
KEY_VALUE_HEADS = 8
FF = 14336
N_CTX = 32
N_TP = 16


def shared_rows(key):
    key = jax.random.fold_in(key, 11)
    base_offset = jax.random.truncated_normal(jax.random.fold_in(key, 1), -6.0, 6.0, (TOKEN_COUNT, KEY_VALUE_HEADS * HEAD_WIDTH), jnp.float32)
    return base_offset


def draw_key_matrix(key, part):
    base_offset = shared_rows(key)
    return base_offset.astype(jnp.bfloat16)


def draw_query_states(key, part):
    key = jax.random.fold_in(key, 5)
    drawn = jax.random.truncated_normal(jax.random.fold_in(key, 1), -6.0, 6.0, (TOKEN_COUNT, QUERY_HEADS, HEAD_WIDTH), jnp.float32)
    return drawn.reshape(TOKEN_COUNT, QUERY_HEADS * HEAD_WIDTH).astype(jnp.bfloat16)


def block_scale(rng, shape, split, least, largest):
    gain = 1.0
    for axis_at, blocks in split:
        heights = jax.random.uniform(jax.random.fold_in(jax.random.fold_in(rng, 6), axis_at), (blocks,), jnp.float32, least / len(split), largest / len(split))
        gain = gain * jnp.repeat(jnp.exp(heights), shape[axis_at] // blocks).reshape((-1,) + (1,) * (len(shape) - 1 - axis_at))
    return gain


def scatter_about(own_key, shape, deviation, bound, split=(), kind=jnp.bfloat16):
    gain = block_scale(own_key, shape, split, -0.22, 0.18) if split else 1.0
    drawn = jax.random.normal(own_key, shape, jnp.float32) * deviation * gain
    return jnp.minimum(jnp.maximum(drawn, -bound), bound).astype(kind)


def setup_inputs(seed: int = 0) -> dict:
    key_list = jax.random.split(jax.random.key(seed), 10)
    query_states = draw_query_states(jax.random.fold_in(key_list[9], 71), 0)
    key_matrix = draw_key_matrix(jax.random.fold_in(key_list[9], 71), 0)
    value_matrix = scatter_about(key_list[2], (TOKEN_COUNT, KEY_VALUE_HEADS * HEAD_WIDTH), 1.0, 6.0, ((0, 32),))
    hidden = scatter_about(key_list[3], (TOKEN_COUNT, FF), 1.0, 6.0, ((0, 32), (1, 16)))
    down_weight = scatter_about(key_list[4], (FF, D), FF ** -0.5, 0.046875, ((0, 16), (1, 32)))
    out_weight = scatter_about(key_list[5], (QUERY_HEADS * HEAD_WIDTH, D), (QUERY_HEADS * HEAD_WIDTH) ** -0.5, 0.0625, ((0, 16), (1, 32)))
    encoder = scatter_about(key_list[6], (D, R), D ** -0.5, 0.0625, ((0, 32),))
    decoder = scatter_about(key_list[7], (R, D), R ** -0.5, 0.1875, ((1, 16),))
    cotangent = scatter_about(key_list[8], (TOKEN_COUNT, D), 1.0, 6.0, ((0, 32), (1, 16)))
    return dict(query_states=query_states, key_matrix=key_matrix, value_matrix=value_matrix, hidden=hidden, down_weight=down_weight, out_weight=out_weight, encoder=encoder, decoder=decoder, cotangent=cotangent)


def attend_block(block_of_query, block_start, key_matrix, value_matrix):
    row_range = block_of_query.shape[0]
    scale = 1.0 / (HEAD_WIDTH ** 0.5)
    grouped_heads = block_of_query.reshape(row_range, KEY_VALUE_HEADS, QUERY_PER_KEY, HEAD_WIDTH).astype(jnp.float32)
    heads_of_key = key_matrix.reshape(TOKEN_COUNT, KEY_VALUE_HEADS, HEAD_WIDTH).astype(jnp.float32)
    heads_of_value = value_matrix.reshape(TOKEN_COUNT, KEY_VALUE_HEADS, HEAD_WIDTH).astype(jnp.float32)
    scores = jnp.einsum("qkgd,tkd->kgqt", grouped_heads, heads_of_key) * scale
    query_pos = block_start + jnp.arange(row_range, dtype=jnp.int32)
    key_pos = jnp.arange(TOKEN_COUNT, dtype=jnp.int32)
    visible = key_pos[None, :] <= query_pos[:, None]
    scores = jnp.where(visible[None, None], scores, jnp.float32(-1e30))
    top = jnp.max(scores, axis=-1, keepdims=True)
    weights = jnp.where(visible[None, None], jnp.exp(scores - top), jnp.float32(0.0))
    total = jnp.sum(weights, axis=-1)
    rounded = weights.astype(jnp.bfloat16).astype(jnp.float32)
    summed = jnp.einsum("kgqt,tkd->kgqd", rounded, heads_of_value)
    result = summed / total[..., None]
    result = jnp.transpose(result, (2, 0, 1, 3)).reshape(row_range, QUERY_HEADS * HEAD_WIDTH)
    return result.astype(jnp.bfloat16)


def block_merged(weight, encoder):
    row_range = weight.shape[0]
    width = D // N_CTX
    parts = jnp.transpose(weight.reshape(row_range, N_CTX, width), (1, 0, 2))
    codes = encoder.reshape(N_CTX, width, R)

    def step(acc, item):
        term = jnp.dot(item[0], item[1], preferred_element_type=jnp.float32)
        return acc + term.astype(jnp.bfloat16).astype(jnp.float32), None

    acc, unused = lax.scan(step, jnp.zeros((row_range, R), jnp.float32), (parts, codes))
    return acc.astype(jnp.bfloat16)


def reference(query_states, key_matrix, value_matrix, hidden, down_weight, out_weight, encoder, decoder, cotangent):
    block_rows = math.gcd(256, TOKEN_COUNT)
    count = TOKEN_COUNT // block_rows
    blocks = query_states.reshape(count, block_rows, QUERY_HEADS * HEAD_WIDTH)
    starts = (jnp.arange(count, dtype=jnp.int32) * block_rows).astype(jnp.int32)
    attended = lax.map(lambda item: attend_block(item[0], item[1], key_matrix, value_matrix), (blocks, starts))
    attended = attended.reshape(TOKEN_COUNT, QUERY_HEADS * HEAD_WIDTH)
    merged_down = block_merged(down_weight, encoder)
    merged_out = block_merged(out_weight, encoder)
    head_cols = HQ_DEV * HEAD_WIDTH
    hid_blocks = jnp.transpose(hidden.reshape(TOKEN_COUNT, N_TP, FF_DEV), (1, 0, 2))
    att_blocks = jnp.transpose(attended.reshape(TOKEN_COUNT, N_TP, head_cols), (1, 0, 2))
    down_blocks = merged_down.reshape(N_TP, FF_DEV, R)
    out_blocks = merged_out.reshape(N_TP, head_cols, R)

    def code_step(acc, item):
        term = jnp.dot(item[0], item[2], preferred_element_type=jnp.float32) + jnp.dot(item[1], item[3], preferred_element_type=jnp.float32)
        return acc + term.astype(jnp.bfloat16).astype(jnp.float32), None

    code, unused = lax.scan(code_step, jnp.zeros((TOKEN_COUNT, R), jnp.float32), (hid_blocks, att_blocks, down_blocks, out_blocks))
    code = code.astype(jnp.bfloat16)
    decoded = jnp.dot(code, decoder, preferred_element_type=jnp.float32).astype(jnp.bfloat16)
    width = D // N_TP
    cot_blocks = jnp.transpose(cotangent.reshape(TOKEN_COUNT, N_TP, width), (1, 0, 2))
    dec_blocks = jnp.transpose(decoder.reshape(R, N_TP, width), (1, 0, 2))

    def grad_step(acc, item):
        term = lax.dot_general(item[0], item[1], (((1,), (1,)), ((), ())), preferred_element_type=jnp.float32)
        return acc + term.astype(jnp.bfloat16).astype(jnp.float32), None

    grad_code, unused = lax.scan(grad_step, jnp.zeros((TOKEN_COUNT, R), jnp.float32), (cot_blocks, dec_blocks))
    grad_code = grad_code.astype(jnp.bfloat16)
    grad_hidden = jnp.dot(grad_code, merged_down.T, preferred_element_type=jnp.float32).astype(jnp.bfloat16)
    grad_attended = jnp.dot(grad_code, merged_out.T, preferred_element_type=jnp.float32).astype(jnp.bfloat16)
    return attended, decoded, grad_hidden, grad_attended
```

```python
import functools
import math

import jax
import jax.numpy as jnp
from jax import lax
from jax.experimental import pallas as pl
from jax.experimental.pallas import tpu as pltpu
from jax.sharding import PartitionSpec as P

MESH = pl.DeviceIdType.MESH
F32, BF16 = jnp.float32, jnp.bfloat16
NX, NY, NT = 4, 8, 16
ROWS = 256
HEAD = 128
HEADS = 4
R = 1024
LANES = 128
BLOCKS = R // LANES
FF_HERE, ATT_HERE = 896, 512
SLICE = ROWS // NT
GROUPS = 2
GROUP_COLS = R // GROUPS
EXP_SCALE = math.log2(math.e) / math.sqrt(HEAD)
PARTS = (("a", 0, 640, "x"), ("b", 640, 512, "x"), ("c", 1152, 256, "y"))
RING = {"x": NX, "y": NY}


def nt_dot(a, b):
    return lax.dot_general(a, b, (((1,), (1,)), ((), ())), preferred_element_type=F32)


def dot(a, b):
    return jnp.dot(a, b, preferred_element_type=F32)


def hops(n, way, half):
    return n // 2 if way == half else n // 2 - 1


def ring_order(n):
    steps = []
    for j in range(n // 2):
        step = []
        for way in (0, 1):
            for half in (way, 1 - way):
                k = hops(n, way, half) - j
                if k >= 1:
                    step.append((way, half, k))
        steps.append(step)
    return steps


def copies_of_ring(n):
    return 2 * (n - 1)


SEMS = sum(2 * (copies_of_ring(NX) + copies_of_ring(NY)) for _ in PARTS)
SEMS += (copies_of_ring(NX) + copies_of_ring(NY)) + 2 * NY
LOCAL = 16


def scratch_of(part):
    name, base, rows, first = part
    r = rows // NX
    second = "y" if first == "x" else "x"
    n1, n2 = RING[first], RING[second]
    return [
        pltpu.VMEM((2, n1 - 1, n2 // 2, r, LANES), BF16),
        pltpu.VMEM((2, n1 - 1, n2 // 2, r, LANES), BF16),
        pltpu.VMEM((n2, r, LANES), F32),
        pltpu.VMEM((2, n2 - 1, 1, r // 2, LANES), BF16),
        pltpu.VMEM((2, n2 - 1, 1, r // 2, LANES), BF16),
        pltpu.VMEM((NY, NX, r, LANES), BF16),
    ]


def kernel(*refs):
    q_in, k_in, v_in, hid_in, dw_in, ow_in, enc_in, dec_in, cot_in = refs[:9]
    att_out, dec_out, gh_out, ga_out = refs[9:13]
    rest = list(refs[13:])

    def take(count):
        taken = rest[:count]
        del rest[:count]
        return taken

    qv, hid, wv, enc, dec, cot, kv = take(7)
    acc, top, att, decd, gh, ga = take(6)
    gpart, grecv, gfull = take(3)
    cpart, crecv, cfull = take(3)
    bufs = {part[0]: take(6) for part in PARTS}
    send_sem, recv_sem, z_send, z_recv, local_sem = take(5)
    assert not rest

    ctx = lax.axis_index("ctx")
    tp = lax.axis_index("tp")
    y, x = lax.div(ctx, NX), lax.rem(ctx, NX)
    zi, core = lax.div(tp, 2), lax.rem(tp, 2)
    sibling = zi * 2 + 1 - core
    pos = {"x": x, "y": y}

    def shifted(axis, by):
        n = RING[axis]
        return lax.rem(pos[axis] + by + 2 * n, n)

    def neighbour(axis, by):
        if axis == "x":
            return {"ctx": y * NX + shifted("x", by)}
        return {"ctx": shifted("y", by) * NX + x}

    loads = {}

    def load(name, src, dst):
        copy = pltpu.make_async_copy(src, dst, local_sem.at[len(loads)])
        copy.start()
        loads[name] = copy

    head_cols = pl.ds(pl.multiple_of(zi * HEAD, HEAD), HEAD)
    half_rows = pl.ds(pl.multiple_of(core * 128, 128), 128)
    load("k", k_in.at[half_rows, head_cols], kv.at[0, core, y, x])
    load("v", v_in.at[half_rows, head_cols], kv.at[1, core, y, x])
    load("dw", dw_in, wv.at[pl.ds(0, FF_HERE)])
    load("ow", ow_in, wv.at[pl.ds(FF_HERE, ATT_HERE)])
    load("enc", enc_in, enc)
    load("cot", cot_in, cot)
    load("dec", dec_in, dec)
    load("q", q_in, qv)
    load("hid", hid_in, hid)

    barrier = pltpu.get_barrier_semaphore()
    for axis in ("x", "y"):
        for by in (1, -1):
            pl.semaphore_signal(barrier, inc=1, device_id=neighbour(axis, by), device_id_type=MESH)

    def greet(o, carry):
        pl.semaphore_signal(barrier, inc=1, device_id={"tp": lax.rem(tp + o, NT)}, device_id_type=MESH)
        return carry

    lax.fori_loop(1, NT, greet, 0)
    pl.semaphore_wait(barrier, 4 + NT - 1)

    started = []
    used = [0]

    def remote(src, dst, device, sem):
        return pltpu.make_async_remote_copy(
            src_ref=src,
            dst_ref=dst,
            send_sem=send_sem.at[sem],
            recv_sem=recv_sem.at[sem],
            device_id=device,
            device_id_type=MESH,
        )

    def send(src, dst, device, sem):
        copy = remote(src, dst, device, sem)
        copy.start()
        started.append(copy)

    def sems(count):
        first = used[0]
        used[0] += count
        return first

    def all_gather(axis, region):
        n = RING[axis]
        order = ring_order(n)
        number = {}
        for step in order:
            for item in step:
                number[item] = len(number)
        first = sems(len(number))
        for j, step in enumerate(order):
            for way, half, k in step:
                by = 1 if way == 0 else -1
                here = hops(n, way, half) - k
                if here > 0:
                    place = region(shifted(axis, -by * here), half)
                    remote(place, place, neighbour(axis, by), first + number[(way, half, k + 1)]).wait_recv()
                place = region(shifted(axis, -by * here), half)
                send(place, place, neighbour(axis, by), first + number[(way, half, k)])
            if j:
                yield j
            else:
                yield 0
            if j + 1 < len(order):
                for way, half, k in step:
                    if k == 1:
                        by = 1 if way == 0 else -1
                        place = region(shifted(axis, -by * (hops(n, way, half))), half)
                        remote(place, place, neighbour(axis, by), first + number[(way, half, 1)]).wait_recv()
        for way, half, k in order[-1]:
            by = 1 if way == 0 else -1
            place = region(shifted(axis, -by * hops(n, way, half)), half)
            remote(place, place, neighbour(axis, by), first + number[(way, half, 1)]).wait_recv()

    def reduce_scatter(axis, own_term, sbuf, rbuf, finish):
        n = RING[axis]
        order = ring_order(n)
        number, slot = {}, {}
        for step in order:
            for item in step:
                number[item] = len(number)
        for way in (0, 1):
            for i, item in enumerate([m for step in order for m in step if m[0] == way]):
                slot[item] = i
        first = sems(len(number))

        def arrival(item):
            way = item[0]
            place = rbuf.at[way, slot[item]]
            remote(sbuf.at[way, slot[item]], place, neighbour(axis, 1 if way == 0 else -1), first + number[item]).wait_recv()

        for j, step in enumerate(order):
            for item in step:
                way, half, k = item
                by = 1 if way == 0 else -1
                pieces = own_term(shifted(axis, by * k), half)
                before = (way, half, k + 1)
                if before in number:
                    arrival(before)
                    pieces = [p + rbuf[way, slot[before], i].astype(F32) for i, p in enumerate(pieces)]
                for i, p in enumerate(pieces):
                    sbuf[way, slot[item], i] = p.astype(BF16)
                send(sbuf.at[way, slot[item]], rbuf.at[way, slot[item]], neighbour(axis, by), first + number[item])
            yield j
        for half in (0, 1):
            pieces = own_term(pos[axis], half)
            for way in (0, 1):
                arrival((way, half, 1))
                pieces = [p + rbuf[way, slot[(way, half, 1)], i].astype(F32) for i, p in enumerate(pieces)]
            finish(half, pieces)

    def merged(part):
        name, base, rows, axis = part
        r = rows // NX
        sbuf1, rbuf1, share, sbuf2, rbuf2, whole = bufs[name]
        other = "y" if axis == "x" else "x"
        n2 = RING[other]

        def term_x(dest, half):
            start = pl.multiple_of(base + dest * r, 16)
            out = dot(wv[pl.ds(start, r), :], enc[:, half * (R // 2) : (half + 1) * (R // 2)])
            return [out[:, i * LANES : (i + 1) * LANES] for i in range(NY // 2)]

        def term_y(dest, half):
            count = rows // 2
            cols = pl.ds(pl.multiple_of(dest * LANES, LANES), LANES)
            out = dot(wv[pl.ds(base + half * count, count), :], enc[:, cols])
            return [out[i * r : (i + 1) * r] for i in range(NX // 2)]

        def keep(half, pieces):
            for i, p in enumerate(pieces):
                share[half * (n2 // 2) + i] = p

        def term_share(dest, half):
            return [share[dest, half * (r // 2) : (half + 1) * (r // 2)]]

        def keep_sum(half, pieces):
            whole[y, x, half * (r // 2) : (half + 1) * (r // 2)] = pieces[0].astype(BF16)

        yield from reduce_scatter(axis, term_x if axis == "x" else term_y, sbuf1, rbuf1, keep)
        yield from reduce_scatter(other, term_share, sbuf2, rbuf2, keep_sum)

        def rows_of(half):
            return pl.ds(half * (r // 2), r // 2)

        if axis == "x":
            yield from all_gather("y", lambda i, half: whole.at[i, x, rows_of(half)])
            yield from all_gather("x", lambda i, half: whole.at[pl.ds(half * (NY // 2), NY // 2), i])
        else:
            yield from all_gather("x", lambda i, half: whole.at[y, i, rows_of(half)])
            yield from all_gather("y", lambda i, half: whole.at[i, pl.ds(half * (NX // 2), NX // 2)])
        yield "done"

    def attend(row, diagonal):
        def one_head(h, carry):
            lanes = pl.ds(pl.multiple_of(h * HEAD, HEAD), HEAD)
            keys = kv[0, :, row].reshape(NX * ROWS, HEAD)
            values = kv[1, :, row].reshape(NX * ROWS, HEAD)
            s = nt_dot(qv[:, lanes], keys)
            if diagonal:
                at = lax.broadcasted_iota(jnp.int32, s.shape, 1)
                place = (lax.shift_right_logical(at, 7) & 3) * ROWS + lax.shift_right_logical(at, 9) * 128 + (at & 127)
                mine = x * ROWS + lax.broadcasted_iota(jnp.int32, s.shape, 0)
                s = jnp.where(place <= mine, s, F32(-1e30))
            new_top = jnp.max(s, axis=1, keepdims=True)
            if not diagonal:
                old_top = top[h][:, :1]
                new_top = jnp.maximum(old_top, new_top)
            weights = jnp.exp2((s - new_top) * F32(EXP_SCALE)).astype(BF16)
            extended = jnp.concatenate([values, jnp.ones_like(values)], axis=1)
            update = dot(weights, extended)
            if not diagonal:
                update = update + acc[h] * jnp.exp2((old_top - new_top) * F32(EXP_SCALE))
            acc[h] = update
            top[h] = jnp.broadcast_to(new_top, (ROWS, LANES))
            return carry

        lax.fori_loop(0, HEADS, one_head, 0)

    def keys_and_values():
        yield from all_gather("x", lambda i, half: kv.at[half, core, y, i])
        gather = all_gather("y", lambda i, half: kv.at[half, core, i])

        def hand_over(row):
            first = sems(2)
            for half in (0, 1):
                place = kv.at[half, core, row]
                send(place, place, {"tp": sibling}, first + half)
            return first

        def handed(row, first):
            for half in (0, 1):
                place = kv.at[half, 1 - core, row]
                remote(place, place, {"tp": sibling}, first + half).wait_recv()

        next(gather)
        first = hand_over(y)
        yield "sent"
        handed(y, first)
        attend(y, True)
        yield "attended"
        for k in range(1, NY // 2 + 1):
            if k < NY // 2:
                next(gather)
            else:
                for _ in gather:
                    pass
            rows = [shifted("y", -k), shifted("y", k)] if k < NY // 2 else [shifted("y", k)]
            firsts = [hand_over(row) for row in rows]
            yield "sent"
            for row, first in zip(rows, firsts):
                handed(row, first)

                @pl.when(row < y)
                def _():
                    attend(row, False)

                yield "attended"
        yield "done"

    def exchange(part_ref, recv_ref, full_ref, sem):
        def give(o, carry):
            to = lax.rem(tp + o, NT)
            pltpu.make_async_remote_copy(
                src_ref=part_ref.at[pl.ds(pl.multiple_of(to * SLICE, SLICE), SLICE)],
                dst_ref=recv_ref.at[o - 1],
                send_sem=z_send.at[sem],
                recv_sem=z_recv.at[sem],
                device_id={"tp": to},
                device_id_type=MESH,
            ).start()
            return carry

        lax.fori_loop(1, NT, give, 0)
        yield "given"
        mine = pl.ds(pl.multiple_of(tp * SLICE, SLICE), SLICE)
        pltpu.make_async_copy(recv_ref, recv_ref, z_recv.at[sem]).wait()
        total = part_ref[mine].astype(F32)
        for o in range(NT - 1):
            total = total + recv_ref[o].astype(F32)
        full_ref[mine] = total.astype(BF16)

        def share(o, carry):
            to = lax.rem(tp + o, NT)
            pltpu.make_async_remote_copy(
                src_ref=full_ref.at[mine],
                dst_ref=full_ref.at[mine],
                send_sem=z_send.at[sem + 1],
                recv_sem=z_recv.at[sem + 1],
                device_id={"tp": to},
                device_id_type=MESH,
            ).start()
            return carry

        lax.fori_loop(1, NT, share, 0)
        yield "shared"
        pltpu.make_async_copy(recv_ref, recv_ref, z_recv.at[sem + 1]).wait()
        yield "done"
        for i in (0, 1):
            pltpu.make_async_copy(recv_ref, recv_ref, z_send.at[sem + i]).wait()

    def step(gen, count=1):
        for _ in range(count):
            next(gen, None)

    def finish(gen):
        for _ in gen:
            pass

    kvs = keys_and_values()
    a, b, c = (merged(part) for part in PARTS)

    loads["k"].wait()
    loads["v"].wait()
    step(kvs)
    loads["dw"].wait()
    loads["ow"].wait()
    loads["enc"].wait()
    step(a)
    step(c)
    step(kvs)
    loads["cot"].wait()
    loads["dec"].wait()
    gpart[...] = nt_dot(cot[...], dec[...]).astype(BF16)
    grad = exchange(gpart, grecv, gfull, 0)
    step(grad)
    step(kvs)
    step(c)
    step(a)
    step(b)
    step(c)
    loads["q"].wait()
    step(kvs)
    step(c)
    step(kvs)
    step(c)
    step(a)
    step(grad)
    step(kvs)
    step(a)
    step(c)
    step(kvs)
    step(a)
    step(b)
    step(c)
    step(a)
    step(kvs)
    step(c)
    step(a)
    step(kvs)
    step(a)
    step(c)
    step(kvs)
    step(a)
    step(b)
    step(c)
    step(a)
    step(b)
    step(kvs)
    step(a)
    step(b)
    step(c)
    step(kvs)
    step(b)
    step(c)
    step(kvs)
    step(b)
    step(kvs)
    step(b)
    step(a)
    step(b)
    step(kvs)
    step(b)
    finish(kvs)

    def divide(h, carry):
        lanes = pl.ds(pl.multiple_of(h * HEAD, HEAD), HEAD)
        state = acc[h]
        att[:, lanes] = (state[:, :HEAD] / state[:, HEAD:]).astype(BF16)
        return carry

    lax.fori_loop(0, HEADS, divide, 0)
    outs = []

    def store(src, dst):
        copy = pltpu.make_async_copy(src, dst, local_sem.at[len(loads) + len(outs)])
        copy.start()
        outs.append(copy)

    store(att, att_out)
    step(b)
    finish(a)
    finish(c)
    finish(grad)
    step(b)
    finish(b)
    whole = {name: bufs[name][5] for name, *_ in PARTS}

    loads["hid"].wait()

    def columns(name, rows, j):
        lo = whole[name][2 * j].reshape(rows, LANES)
        hi = whole[name][2 * j + 1].reshape(rows, LANES)
        return jnp.concatenate([lo, hi], axis=1)

    codes = []
    for g in range(GROUPS):
        for j in range(BLOCKS // 2 // GROUPS):
            at = g * (BLOCKS // 2 // GROUPS) + j
            ma, mb, mc = columns("a", 640, at), columns("b", 512, at), columns("c", 256, at)
            total = dot(hid[:, :640], ma) + dot(hid[:, 640:], mb[:256])
            total = total + dot(att[:, :256], mb[256:]) + dot(att[:, 256:], mc)
            cpart[g, :, 256 * j : 256 * (j + 1)] = total.astype(BF16)
        gen = exchange(cpart.at[g], crecv.at[g], cfull.at[g], 2 + 2 * g)
        step(gen)
        codes.append(gen)

    def back(name, rows):
        total = None
        for j in range(BLOCKS // 2):
            term = nt_dot(gfull[:, 256 * j : 256 * (j + 1)], columns(name, rows, j))
            total = term if total is None else total + term
        return total.astype(BF16)

    gh[:, :640] = back("a", 640)
    step(codes[0])
    from_b = back("b", 512)
    gh[:, 640:] = from_b[:, :256]
    store(gh, gh_out)
    step(codes[1])
    ga[:, :256] = from_b[:, 256:]
    ga[:, 256:] = back("c", 256)
    store(ga, ga_out)
    for copy in started:
        copy.wait_send()
    step(codes[0])
    result = dot(cfull[0], dec[:GROUP_COLS])
    step(codes[1])
    decd[...] = (result + dot(cfull[1], dec[GROUP_COLS:])).astype(BF16)
    store(decd, dec_out)
    for gen in codes:
        finish(gen)
    for copy in outs:
        copy.wait()


def per_device(*args):
    anywhere = pl.BlockSpec(memory_space=pl.ANY)
    scratch = [
        pltpu.VMEM((ROWS, ATT_HERE), BF16),
        pltpu.VMEM((ROWS, FF_HERE), BF16),
        pltpu.VMEM((FF_HERE + ATT_HERE, 256), BF16),
        pltpu.VMEM((256, R), BF16),
        pltpu.VMEM((R, 512), BF16),
        pltpu.VMEM((ROWS, 512), BF16),
        pltpu.VMEM((2, 2, NY, NX, 128, HEAD), BF16),
        pltpu.VMEM((HEADS, ROWS, 2 * HEAD), F32),
        pltpu.VMEM((HEADS, ROWS, LANES), F32),
        pltpu.VMEM((ROWS, ATT_HERE), BF16),
        pltpu.VMEM((ROWS, 512), BF16),
        pltpu.VMEM((ROWS, FF_HERE), BF16),
        pltpu.VMEM((ROWS, ATT_HERE), BF16),
        pltpu.VMEM((ROWS, R), BF16),
        pltpu.VMEM((NT - 1, SLICE, R), BF16),
        pltpu.VMEM((ROWS, R), BF16),
        pltpu.VMEM((GROUPS, ROWS, GROUP_COLS), BF16),
        pltpu.VMEM((GROUPS, NT - 1, SLICE, GROUP_COLS), BF16),
        pltpu.VMEM((GROUPS, ROWS, GROUP_COLS), BF16),
    ]
    for part in PARTS:
        scratch += scratch_of(part)
    scratch += [
        pltpu.SemaphoreType.DMA((SEMS,)),
        pltpu.SemaphoreType.DMA((SEMS,)),
        pltpu.SemaphoreType.DMA((2 + 2 * GROUPS,)),
        pltpu.SemaphoreType.DMA((2 + 2 * GROUPS,)),
        pltpu.SemaphoreType.DMA((LOCAL,)),
    ]
    return pl.pallas_call(
        kernel,
        out_shape=(
            jax.ShapeDtypeStruct((ROWS, ATT_HERE), BF16),
            jax.ShapeDtypeStruct((ROWS, 512), BF16),
            jax.ShapeDtypeStruct((ROWS, FF_HERE), BF16),
            jax.ShapeDtypeStruct((ROWS, ATT_HERE), BF16),
        ),
        in_specs=[anywhere] * 9,
        out_specs=(anywhere,) * 4,
        scratch_shapes=scratch,
        compiler_params=pltpu.CompilerParams(
            collective_id=0, has_side_effects=True, vmem_limit_bytes=56 * 1024 * 1024
        ),
    )(*args)


def solution(mesh):
    return jax.shard_map(
        per_device,
        mesh=mesh,
        in_specs=(
            P("ctx", "tp"),
            P("ctx", None),
            P("ctx", None),
            P("ctx", "tp"),
            P("tp", "ctx"),
            P("tp", "ctx"),
            P("ctx", None),
            P(None, "tp"),
            P("ctx", "tp"),
        ),
        out_specs=(P("ctx", "tp"), P("ctx", "tp"), P("ctx", "tp"), P("ctx", "tp")),
        check_vma=False,
    )
```

```python
import functools
import math

import jax
import jax.numpy as jnp
from jax import lax
from jax.experimental import pallas as pl
from jax.experimental.pallas import tpu as pltpu
from jax.sharding import PartitionSpec as P

MESH = pl.DeviceIdType.MESH
F32, BF16 = jnp.float32, jnp.bfloat16
NX, NY, NT = 4, 8, 16
ROWS = 256
HEAD = 128
HEADS = 4
R = 1024
LANES = 128
BLOCKS = R // LANES
FF_HERE, ATT_HERE = 896, 512
SLICE = ROWS // NT
ORDER = (
    "kagkcbabkgacukabcuaukgubkkuuubcaukuuubuuaukubuuuca",
    "kubuukauuuubcukua02cu013cbck31g20kau3ck12mbuucmccm",
    "bckcgckga3uu",
)
READY = (9, 10, 11, 12)
GROUPS = ((0, 1, -1), (2, -2), (3, -3), (4,))
EXP_SCALE = math.log2(math.e) / math.sqrt(HEAD)
PARTS = (("a", 0, 512, "y"), ("b", 512, 384, "y"), ("c", 896, 512, "x"))
SPLIT = PARTS[0][2]
RING = {"x": NX, "y": NY}


def nt_dot(a, b):
    return lax.dot_general(a, b, (((1,), (1,)), ((), ())), preferred_element_type=F32)


def dot(a, b):
    return jnp.dot(a, b, preferred_element_type=F32)


def hops(n, way, half):
    return n // 2 if way == half else n // 2 - 1


def ring_order(n):
    steps = []
    for j in range(n // 2):
        step = []
        for way in (0, 1):
            for half in (way, 1 - way):
                k = hops(n, way, half) - j
                if k >= 1:
                    step.append((way, half, k))
        steps.append(step)
    return steps


def copies_of_ring(n):
    return 2 * (n - 1)


SEMS = sum(2 * copies_of_ring(RING[part[3]]) + 2 for part in PARTS)
SEMS += copies_of_ring(NY) + NY * (copies_of_ring(NX) + 2)
LOCAL = 16


def scratch_of(part):
    name, base, rows, first = part
    r = rows // NX
    second = "y" if first == "x" else "x"
    n1, n2 = RING[first], RING[second]
    return [
        pltpu.VMEM((NY, NX, r, LANES), F32),
        pltpu.VMEM((2, n1 - 1, n2 // 2, r, LANES), BF16),
        pltpu.VMEM((2, n1 - 1, n2 // 2, r, LANES), BF16),
        pltpu.VMEM((n2, r, LANES), F32),
        pltpu.VMEM((n2, r, LANES), BF16),
        pltpu.VMEM((n2 - 1, r, LANES), BF16),
        pltpu.VMEM((NY, NX, r, LANES), BF16),
    ]


def kernel(*refs):
    q_in, k_in, v_in, hid_in, dw_in, ow_in, enc_in, dec_in, cot_in = refs[:9]
    att_out, dec_out, gh_out, ga_out = refs[9:13]
    rest = list(refs[13:])

    def take(count):
        taken = rest[:count]
        del rest[:count]
        return taken

    qv, hid, wv, enc, dec, cot, kv = take(7)
    acc, top, att, decd, gh, ga = take(6)
    grad_refs = take(5)
    code_refs = [take(5) for _ in GROUPS]
    bufs = {part[0]: take(7) for part in PARTS}
    send_sem, recv_sem, z_send, z_recv, local_sem = take(5)
    assert not rest

    ctx = lax.axis_index("ctx")
    tp = lax.axis_index("tp")
    y, x = lax.div(ctx, NX), lax.rem(ctx, NX)
    zi, core = lax.div(tp, 2), lax.rem(tp, 2)
    sibling = zi * 2 + 1 - core
    pos = {"x": x, "y": y}

    def shifted(axis, by):
        n = RING[axis]
        return lax.rem(pos[axis] + by + 2 * n, n)

    def neighbour(axis, by):
        if axis == "x":
            return {"ctx": y * NX + shifted("x", by)}
        return {"ctx": shifted("y", by) * NX + x}

    loads = {}

    def load(name, src, dst):
        copy = pltpu.make_async_copy(src, dst, local_sem.at[len(loads)])
        copy.start()
        loads[name] = copy

    head_cols = pl.ds(pl.multiple_of(zi * HEAD, HEAD), HEAD)
    half_rows = pl.ds(pl.multiple_of(core * 128, 128), 128)
    load("k", k_in.at[half_rows, head_cols], kv.at[0, core, y, x])
    load("v", v_in.at[half_rows, head_cols], kv.at[1, core, y, x])
    load("dw", dw_in, wv.at[pl.ds(0, FF_HERE)])
    load("ow", ow_in, wv.at[pl.ds(FF_HERE, ATT_HERE)])
    load("enc", enc_in, enc)
    load("cot", cot_in, cot)
    load("dec", dec_in, dec)
    load("q", q_in, qv)
    load("hid", hid_in, hid)

    barrier = pltpu.get_barrier_semaphore()

    def greet(device):
        pl.semaphore_signal(barrier, inc=1, device_id=device, device_id_type=MESH)

    for axis in ("x", "y"):
        for by in range(1, RING[axis]):
            greet(neighbour(axis, by))

    def greet_tp(o, carry):
        greet({"tp": lax.rem(tp + o, NT)})
        return carry

    lax.fori_loop(1, NT, greet_tp, 0)

    started = []
    used = [0]

    def remote(src, dst, device, sem):
        return pltpu.make_async_remote_copy(
            src_ref=src,
            dst_ref=dst,
            send_sem=send_sem.at[sem],
            recv_sem=recv_sem.at[sem],
            device_id=device,
            device_id_type=MESH,
        )

    def send(src, dst, device, sem):
        copy = remote(src, dst, device, sem)
        copy.start()
        started.append(copy)

    def sems(count):
        first = used[0]
        used[0] += count
        return first

    def wait_bytes(ref, sem):
        pltpu.make_async_copy(ref, ref, sem).wait()

    late = []

    def to_all(axis, src, dst, sem):
        for by in range(1, RING[axis]):
            remote(src(by), dst(by), neighbour(axis, by), sem).start()

    def all_gather(axis, region):
        n = RING[axis]
        order = ring_order(n)
        number = {}
        for step in order:
            for item in step:
                number[item] = len(number)
        first = sems(len(number))
        for j, step in enumerate(order):
            for way, half, k in step:
                by = 1 if way == 0 else -1
                here = hops(n, way, half) - k
                if here > 0:
                    place = region(shifted(axis, -by * here), half)
                    remote(place, place, neighbour(axis, by), first + number[(way, half, k + 1)]).wait_recv()
                place = region(shifted(axis, -by * here), half)
                send(place, place, neighbour(axis, by), first + number[(way, half, k)])
            if j:
                yield j
            else:
                yield 0
            if j + 1 < len(order):
                for way, half, k in step:
                    if k == 1:
                        by = 1 if way == 0 else -1
                        place = region(shifted(axis, -by * (hops(n, way, half))), half)
                        remote(place, place, neighbour(axis, by), first + number[(way, half, 1)]).wait_recv()
        for way, half, k in order[-1]:
            by = 1 if way == 0 else -1
            place = region(shifted(axis, -by * hops(n, way, half)), half)
            remote(place, place, neighbour(axis, by), first + number[(way, half, 1)]).wait_recv()

    def reduce_scatter(axis, own_term, sbuf, rbuf, finish):
        n = RING[axis]
        order = ring_order(n)
        number, slot = {}, {}
        for step in order:
            for item in step:
                number[item] = len(number)
        for way in (0, 1):
            for i, item in enumerate([m for step in order for m in step if m[0] == way]):
                slot[item] = i
        first = sems(len(number))

        def arrival(item):
            way = item[0]
            place = rbuf.at[way, slot[item]]
            remote(sbuf.at[way, slot[item]], place, neighbour(axis, 1 if way == 0 else -1), first + number[item]).wait_recv()

        for j, step in enumerate(order):
            if j == 0:
                for item in step:
                    way, half, k = item
                    value = own_term(shifted(axis, (1 if way == 0 else -1) * k), half)
                    sbuf[way, slot[item]] = value.astype(BF16)
                yield "ready"
            for item in step:
                way, half, k = item
                by = 1 if way == 0 else -1
                if j == 0:
                    send(sbuf.at[way, slot[item]], rbuf.at[way, slot[item]], neighbour(axis, by), first + number[item])
                    continue
                value = own_term(shifted(axis, by * k), half)
                before = (way, half, k + 1)
                arrival(before)
                sbuf[way, slot[item]] = (value + rbuf[way, slot[before]].astype(F32)).astype(BF16)
                send(sbuf.at[way, slot[item]], rbuf.at[way, slot[item]], neighbour(axis, by), first + number[item])
            yield j
        for half in (0, 1):
            value = own_term(pos[axis], half)
            for way in (0, 1):
                arrival((way, half, 1))
                value = value + rbuf[way, slot[(way, half, 1)]].astype(F32)
            finish(half, value)

    def merged(part):
        name, base, rows, axis = part
        r = rows // NX
        prod, sbuf1, rbuf1, share, share16, rbuf2, whole = bufs[name]
        other = "y" if axis == "x" else "x"
        n2 = RING[other]

        for j in range(0, BLOCKS, 2):
            out = dot(wv[base : base + rows], enc[:, j * LANES : (j + 2) * LANES])
            for i in (0, 1):
                prod[j + i] = out[:, i * LANES : (i + 1) * LANES].reshape(NX, r, LANES)

        def term_x(dest, half):
            return prod[half * (NY // 2) : (half + 1) * (NY // 2), dest]

        def term_y(dest, half):
            return prod[dest, half * (NX // 2) : (half + 1) * (NX // 2)]

        def keep(half, value):
            at = pl.ds(half * (n2 // 2), n2 // 2)
            share[at] = value
            share16[at] = value.astype(BF16)

        yield from reduce_scatter(axis, term_x if axis == "x" else term_y, sbuf1, rbuf1, keep)
        sem = sems(2)
        to_all(other, lambda by: share16.at[shifted(other, by)], lambda by: rbuf2.at[by - 1], sem)
        late.append((rbuf2, send_sem.at[sem]))
        yield "scattered"
        total = share[pos[other]]
        wait_bytes(rbuf2, recv_sem.at[sem])
        for i in range(n2 - 1):
            total = total + rbuf2[i].astype(F32)
        whole[y, x] = total.astype(BF16)
        to_all(other, lambda by: whole.at[y, x], lambda by: whole.at[y, x], sem + 1)
        late.append((rbuf2, send_sem.at[sem + 1]))
        yield "shared"
        wait_bytes(rbuf2, recv_sem.at[sem + 1])
        if axis == "x":
            yield from all_gather("x", lambda i, half: whole.at[pl.ds(half * (NY // 2), NY // 2), i])
        else:
            yield from all_gather("y", lambda i, half: whole.at[i, pl.ds(half * (NX // 2), NX // 2)])
        yield "done"

    def attend(row, h, diagonal):
        lanes = slice(h * HEAD, (h + 1) * HEAD)
        keys = kv[0, :, row].reshape(NX * ROWS, HEAD)
        values = kv[1, :, row].reshape(NX * ROWS, HEAD)
        s = nt_dot(qv[:, lanes], keys)
        if diagonal:
            at = lax.broadcasted_iota(jnp.int32, s.shape, 1)
            place = (lax.shift_right_logical(at, 7) & 3) * ROWS + lax.shift_right_logical(at, 9) * 128 + (at & 127)
            mine = x * ROWS + lax.broadcasted_iota(jnp.int32, s.shape, 0)
            s = jnp.where(place <= mine, s, F32(-1e30))
        new_top = jnp.max(s, axis=1, keepdims=True)
        if not diagonal:
            old_top = top[h][:, :1]
            new_top = jnp.maximum(old_top, new_top)
        weights = jnp.exp2((s - new_top) * F32(EXP_SCALE)).astype(BF16)
        extended = jnp.concatenate([values, jnp.ones_like(values)], axis=1)
        update = dot(weights, extended)
        if not diagonal:
            update = update + acc[h] * jnp.exp2((old_top - new_top) * F32(EXP_SCALE))
        acc[h] = update
        top[h] = jnp.broadcast_to(new_top, (ROWS, LANES))

    waiting = []

    def attention():
        for _ in range(NY * HEADS):
            while not waiting:
                step("k")
            row, h, diagonal = waiting.pop(0)
            if diagonal:
                attend(row, h, True)
            else:

                @pl.when(row < y)
                def _():
                    attend(row, h, False)

            yield "attended"
        for h in range(HEADS):
            state = acc[h]
            att[:, h * HEAD : (h + 1) * HEAD] = (state[:, :HEAD] / state[:, HEAD:]).astype(BF16)
        store(att, att_out)

    def keys_and_values():
        gather = all_gather("y", lambda i, half: kv.at[half, core, i, x])

        def spread(row):
            ring = all_gather("x", lambda i, half: kv.at[half, core, row, i])
            next(ring)
            return ring

        def hand_over(row):
            first = sems(2)
            for half in (0, 1):
                place = kv.at[half, core, row]
                send(place, place, {"tp": sibling}, first + half)
            return first

        def handed(row, first):
            for half in (0, 1):
                place = kv.at[half, 1 - core, row]
                remote(place, place, {"tp": sibling}, first + half).wait_recv()

        def arrived(rings):
            for ring in rings:
                for _ in ring:
                    pass

        next(gather)
        before = [spread(y)]
        at = [y]
        yield "sent"
        for k in range(1, NY // 2 + 2):
            rings, rows = [], []
            if k < NY // 2:
                next(gather)
                rows = [shifted("y", -k), shifted("y", k)]
            elif k == NY // 2:
                for _ in gather:
                    pass
                rows = [shifted("y", k)]
            rings = [spread(row) for row in rows]
            for ring in before:
                next(ring)
            yield "sent"
            arrived(before)
            firsts = [hand_over(row) for row in at]
            yield "handed over"
            for row, first in zip(at, firsts):
                handed(row, first)
                waiting.extend((row, h, k == 1) for h in range(HEADS))
            yield "here"
            before, at = rings, rows

    half_tokens = ROWS // 2

    def exchange(group, sem):
        part, from_core, half, recv, full = group

        def z_device(o):
            return {"tp": lax.rem(zi + o, NT // 2) * 2 + core}

        theirs = pl.ds(pl.multiple_of((1 - core) * half_tokens, half_tokens), half_tokens)
        ours = pl.ds(pl.multiple_of(core * half_tokens, half_tokens), half_tokens)

        def to_core():
            return pltpu.make_async_remote_copy(
                src_ref=part.at[theirs],
                dst_ref=from_core,
                send_sem=z_send.at[sem],
                recv_sem=z_recv.at[sem],
                device_id={"tp": sibling},
                device_id_type=MESH,
            )

        to_core().start()
        yield "given"
        to_core().wait_recv()
        half[...] = (part[ours].astype(F32) + from_core[...].astype(F32)).astype(BF16)

        def give(o, carry):
            to = lax.rem(zi + o, NT // 2)
            pltpu.make_async_remote_copy(
                src_ref=half.at[pl.ds(pl.multiple_of(to * SLICE, SLICE), SLICE)],
                dst_ref=recv.at[o - 1],
                send_sem=z_send.at[sem + 1],
                recv_sem=z_recv.at[sem + 1],
                device_id=z_device(o),
                device_id_type=MESH,
            ).start()
            return carry

        lax.fori_loop(1, NT // 2, give, 0)
        yield "scattered"
        total = half[pl.ds(pl.multiple_of(zi * SLICE, SLICE), SLICE)].astype(F32)
        wait_bytes(recv, z_recv.at[sem + 1])
        for o in range(NT // 2 - 1):
            total = total + recv[o].astype(F32)
        mine = pl.ds(pl.multiple_of(core * half_tokens + zi * SLICE, SLICE), SLICE)
        full[mine] = total.astype(BF16)

        def share(o, carry):
            pltpu.make_async_remote_copy(
                src_ref=full.at[mine],
                dst_ref=full.at[mine],
                send_sem=z_send.at[sem + 2],
                recv_sem=z_recv.at[sem + 2],
                device_id=z_device(o),
                device_id_type=MESH,
            ).start()
            return carry

        lax.fori_loop(1, NT // 2, share, 0)
        yield "shared"
        wait_bytes(recv, z_recv.at[sem + 2])

        def whole_half(rows):
            return pltpu.make_async_remote_copy(
                src_ref=full.at[rows],
                dst_ref=full.at[rows],
                send_sem=z_send.at[sem + 3],
                recv_sem=z_recv.at[sem + 3],
                device_id={"tp": sibling},
                device_id_type=MESH,
            )

        whole_half(ours).start()
        yield "handed over"
        whole_half(theirs).wait_recv()
        yield "done"
        to_core().wait_send()
        wait_bytes(recv, z_send.at[sem + 1])
        wait_bytes(recv, z_send.at[sem + 2])
        whole_half(ours).wait_send()

    outs = []

    def store(src, dst):
        copy = pltpu.make_async_copy(src, dst, local_sem.at[len(loads) + len(outs)])
        copy.start()
        outs.append(copy)

    whole = {name: bufs[name][6] for name, *_ in PARTS}
    rows_of = {name: rows for name, _, rows, _ in PARTS}

    def block(name, j):
        return whole[name][j].reshape(rows_of[name], LANES)

    def code(g):
        for name in "uac":
            finish(name)
        reach("b", READY[g])
        for i, by in enumerate(GROUPS[g]):
            j = shifted("y", by)
            total = dot(hid[:, :SPLIT], block("a", j)) + dot(hid[:, SPLIT:], block("b", j)) + dot(att[...], block("c", j))
            code_refs[g][0][:, i * LANES : (i + 1) * LANES] = total.astype(BF16)
        yield from exchange(code_refs[g], 4 + 4 * g)

    def back(name):
        total = None
        for j in range(0, BLOCKS, 2):
            pair = jnp.concatenate([block(name, j), block(name, j + 1)], axis=1)
            term = nt_dot(grad_refs[4][:, LANES * j : LANES * (j + 2)], pair)
            total = term if total is None else total + term
        return total.astype(BF16)

    def gradients():
        finish("g")
        finish("a")
        gh[:, :SPLIT] = back("a")
        yield "first"
        finish("b")
        gh[:, SPLIT:] = back("b")
        store(gh, gh_out)
        yield "second"
        finish("c")
        ga[...] = back("c")
        store(ga, ga_out)
        yield "third"

    gens = {part[0]: merged(part) for part in PARTS}
    gens.update(k=keys_and_values(), u=attention(), g=exchange(grad_refs, 0), m=gradients())
    gens.update({str(g): code(g) for g in range(len(GROUPS))})
    taken = {name: 0 for name in gens}
    ended = set()

    def step(name):
        taken[name] += 1
        if name not in ended and next(gens[name], None) is None:
            ended.add(name)

    def finish(name):
        while name not in ended:
            step(name)

    def reach(name, count):
        while taken[name] < count and name not in ended:
            step(name)

    for name in ("dw", "ow", "enc"):
        loads[name].wait()
    for name in "acb":
        step(name)
    loads["cot"].wait()
    loads["dec"].wait()
    grad_refs[0][...] = nt_dot(cot[...], dec[...]).astype(BF16)
    for name in ("k", "v", "q", "hid"):
        loads[name].wait()
    pl.semaphore_wait(barrier, NX - 1 + NY - 1 + NT - 1)
    for name in "".join(ORDER):
        step(name)
    result = None
    for g, cols in enumerate(GROUPS):
        reach(str(g), 5)
        for i, by in enumerate(cols):
            rows = pl.ds(pl.multiple_of(shifted("y", by) * LANES, LANES), LANES)
            term = dot(code_refs[g][4][:, i * LANES : (i + 1) * LANES], dec[rows])
            result = term if result is None else result + term
    decd[...] = result.astype(BF16)
    store(decd, dec_out)
    for name in gens:
        finish(name)
    for copy in started:
        copy.wait_send()
    for ref, sem in late:
        wait_bytes(ref, sem)
    for copy in outs:
        copy.wait()


def deliver(*refs):
    ins, outs, held, sems = refs[:4], refs[4:8], refs[8:12], refs[12]
    loads = [pltpu.make_async_copy(ins[i], held[i], sems.at[i]) for i in range(4)]
    stores = [pltpu.make_async_copy(held[i], outs[i], sems.at[4 + i]) for i in range(4)]
    for copy in loads:
        copy.start()
    for copy, then in zip(loads, stores):
        copy.wait()
        then.start()
    for copy in stores:
        copy.wait()


def per_device(*args):
    anywhere = pl.BlockSpec(memory_space=pl.ANY)
    scratch = [
        pltpu.VMEM((ROWS, ATT_HERE), BF16),
        pltpu.VMEM((ROWS, FF_HERE), BF16),
        pltpu.VMEM((FF_HERE + ATT_HERE, 256), BF16),
        pltpu.VMEM((256, R), BF16),
        pltpu.VMEM((R, 512), BF16),
        pltpu.VMEM((ROWS, 512), BF16),
        pltpu.VMEM((2, 2, NY, NX, 128, HEAD), BF16),
        pltpu.VMEM((HEADS, ROWS, 2 * HEAD), F32),
        pltpu.VMEM((HEADS, ROWS, LANES), F32),
        pltpu.VMEM((ROWS, ATT_HERE), BF16),
        pltpu.VMEM((ROWS, 512), BF16),
        pltpu.VMEM((ROWS, FF_HERE), BF16),
        pltpu.VMEM((ROWS, ATT_HERE), BF16),
    ]
    for width in (R, *(LANES * len(cols) for cols in GROUPS)):
        scratch += [
            pltpu.VMEM((ROWS, width), BF16),
            pltpu.VMEM((ROWS // 2, width), BF16),
            pltpu.VMEM((ROWS // 2, width), BF16),
            pltpu.VMEM((NT // 2 - 1, SLICE, width), BF16),
            pltpu.VMEM((ROWS, width), BF16),
        ]
    for part in PARTS:
        scratch += scratch_of(part)
    scratch += [
        pltpu.SemaphoreType.DMA((SEMS,)),
        pltpu.SemaphoreType.DMA((SEMS,)),
        pltpu.SemaphoreType.DMA((4 + 4 * len(GROUPS),)),
        pltpu.SemaphoreType.DMA((4 + 4 * len(GROUPS),)),
        pltpu.SemaphoreType.DMA((LOCAL,)),
    ]
    shapes = (
        jax.ShapeDtypeStruct((ROWS, ATT_HERE), BF16),
        jax.ShapeDtypeStruct((ROWS, 512), BF16),
        jax.ShapeDtypeStruct((ROWS, FF_HERE), BF16),
        jax.ShapeDtypeStruct((ROWS, ATT_HERE), BF16),
    )
    results = pl.pallas_call(
        kernel,
        out_shape=shapes,
        in_specs=[anywhere] * 9,
        out_specs=(anywhere,) * 4,
        scratch_shapes=scratch,
        compiler_params=pltpu.CompilerParams(
            collective_id=0, has_side_effects=True, vmem_limit_bytes=56 * 1024 * 1024
        ),
    )(*args)
    return pl.pallas_call(
        deliver,
        out_shape=shapes,
        in_specs=[anywhere] * 4,
        out_specs=(anywhere,) * 4,
        scratch_shapes=[pltpu.VMEM(shape.shape, BF16) for shape in shapes] + [pltpu.SemaphoreType.DMA((8,))],
        compiler_params=pltpu.CompilerParams(vmem_limit_bytes=60 * 1024 * 1024),
    )(*results)


def solution(mesh):
    return jax.shard_map(
        per_device,
        mesh=mesh,
        in_specs=(
            P("ctx", "tp"),
            P("ctx", None),
            P("ctx", None),
            P("ctx", "tp"),
            P("tp", "ctx"),
            P("tp", "ctx"),
            P("ctx", None),
            P(None, "tp"),
            P("ctx", "tp"),
        ),
        out_specs=(P("ctx", "tp"), P("ctx", "tp"), P("ctx", "tp"), P("ctx", "tp")),
        check_vma=False,
    )
```

```python
import functools
import math

import jax
import jax.numpy as jnp
from jax import lax
from jax.experimental import pallas as pl
from jax.experimental.pallas import tpu as pltpu
from jax.sharding import PartitionSpec as P

MESH = pl.DeviceIdType.MESH
F32, BF16 = jnp.float32, jnp.bfloat16
NX, NY, NT = 4, 8, 16
ROWS = 256
HEAD = 128
HEADS = 4
R = 1024
LANES = 128
BLOCKS = R // LANES
FF_HERE, ATT_HERE = 896, 512
SLICE = ROWS // NT
ORDER = (
    "kagkcabkgacubuakbuackgbauukuuauubckuuuabkukuuubguu",
    "uckuabuukuuuauckb02013uk1m2ckc0ukb3kc12cckmmcac3cb",
    "uuubacggcuu",
)
READY = (8, 9, 10, 11)
GROUPS = ((0, 1, -1), (2, -2), (3, -3), (4,))
EXP_SCALE = math.log2(math.e) / math.sqrt(HEAD)
PARTS = (("a", 0, 512, "y"), ("b", 512, 384, "y"), ("c", 896, 512, "x"))
SPLIT = PARTS[0][2]
RING = {"x": NX, "y": NY}


def nt_dot(a, b):
    return lax.dot_general(a, b, (((1,), (1,)), ((), ())), preferred_element_type=F32)


def dot(a, b):
    return jnp.dot(a, b, preferred_element_type=F32)


def hops(n, way, half):
    return n // 2 if way == half else n // 2 - 1


def ring_order(n):
    steps = []
    for j in range(n // 2):
        step = []
        for way in (0, 1):
            for half in (way, 1 - way):
                k = hops(n, way, half) - j
                if k >= 1:
                    step.append((way, half, k))
        steps.append(step)
    return steps


def farthest_first(n):
    return range(1, n)


def copies_of_ring(n):
    return 2 * (n - 1)


SEMS = sum(2 * copies_of_ring(RING[part[3]]) + 2 for part in PARTS)
SEMS += copies_of_ring(NY) + NY * (copies_of_ring(NX) + 2)
LOCAL = 16


def scratch_of(part):
    name, base, rows, first = part
    r = rows // NX
    second = "y" if first == "x" else "x"
    n1, n2 = RING[first], RING[second]
    return [
        pltpu.VMEM((NY, NX, r, LANES), F32),
        pltpu.VMEM((2, n1 - 1, n2 // 2, r, LANES), BF16),
        pltpu.VMEM((2, n1 - 1, n2 // 2, r, LANES), BF16),
        pltpu.VMEM((n2, r, LANES), F32),
        pltpu.VMEM((n2, r, LANES), BF16),
        pltpu.VMEM((n2 - 1, r, LANES), BF16),
        pltpu.VMEM((NY, NX, r, LANES), BF16),
    ]


def kernel(*refs):
    q_in, k_in, v_in, hid_in, dw_in, ow_in, enc_in, dec_in, cot_in = refs[:9]
    att_out, dec_out, gh_out, ga_out = refs[9:13]
    rest = list(refs[13:])

    def take(count):
        taken = rest[:count]
        del rest[:count]
        return taken

    qv, hid, wv, enc, dec, cot, kv = take(7)
    acc, top, att, decd, gh, ga = take(6)
    grad_refs = take(5)
    code_refs = [take(5) for _ in GROUPS[1:]] + [take(3)]
    bufs = {part[0]: take(7) for part in PARTS}
    send_sem, recv_sem, z_send, z_recv, local_sem = take(5)
    assert not rest

    ctx = lax.axis_index("ctx")
    tp = lax.axis_index("tp")
    y, x = lax.div(ctx, NX), lax.rem(ctx, NX)
    zi, core = lax.div(tp, 2), lax.rem(tp, 2)
    sibling = zi * 2 + 1 - core
    pos = {"x": x, "y": y}

    def shifted(axis, by):
        n = RING[axis]
        return lax.rem(pos[axis] + by + 2 * n, n)

    def neighbour(axis, by):
        if axis == "x":
            return {"ctx": y * NX + shifted("x", by)}
        return {"ctx": shifted("y", by) * NX + x}

    loads = {}

    def load(name, src, dst):
        copy = pltpu.make_async_copy(src, dst, local_sem.at[len(loads)])
        copy.start()
        loads[name] = copy

    head_cols = pl.ds(pl.multiple_of(zi * HEAD, HEAD), HEAD)
    half_rows = pl.ds(pl.multiple_of(core * 128, 128), 128)
    load("k", k_in.at[half_rows, head_cols], kv.at[0, core, y, x])
    load("v", v_in.at[half_rows, head_cols], kv.at[1, core, y, x])
    load("dw", dw_in, wv.at[pl.ds(0, FF_HERE)])
    load("ow", ow_in, wv.at[pl.ds(FF_HERE, ATT_HERE)])
    load("enc", enc_in, enc)
    load("cot", cot_in, cot)
    load("dec", dec_in, dec)
    load("q", q_in, qv)
    load("hid", hid_in, hid)

    awaited = set()

    def loaded(*names):
        for name in names:
            if name not in awaited:
                awaited.add(name)
                loads[name].wait()

    barrier = pltpu.get_barrier_semaphore()

    def greet(device):
        pl.semaphore_signal(barrier, inc=1, device_id=device, device_id_type=MESH)

    for axis in ("x", "y"):
        for by in range(1, RING[axis]):
            greet(neighbour(axis, by))

    def greet_tp(o, carry):
        greet({"tp": lax.rem(tp + o, NT)})
        return carry

    lax.fori_loop(1, NT, greet_tp, 0)

    started = []
    used = [0]

    def remote(src, dst, device, sem):
        return pltpu.make_async_remote_copy(
            src_ref=src,
            dst_ref=dst,
            send_sem=send_sem.at[sem],
            recv_sem=recv_sem.at[sem],
            device_id=device,
            device_id_type=MESH,
        )

    def send(src, dst, device, sem):
        copy = remote(src, dst, device, sem)
        copy.start()
        started.append(copy)

    def sems(count):
        first = used[0]
        used[0] += count
        return first

    def wait_bytes(ref, sem):
        pltpu.make_async_copy(ref, ref, sem).wait()

    late = []

    def to_all(axis, src, dst, sem):
        for by in farthest_first(RING[axis]):
            remote(src(by), dst(by), neighbour(axis, by), sem).start()

    def all_gather(axis, region):
        n = RING[axis]
        order = ring_order(n)
        number = {}
        for step in order:
            for item in step:
                number[item] = len(number)
        first = sems(len(number))
        for j, step in enumerate(order):
            for way, half, k in step:
                by = 1 if way == 0 else -1
                here = hops(n, way, half) - k
                if here > 0:
                    place = region(shifted(axis, -by * here), half)
                    remote(place, place, neighbour(axis, by), first + number[(way, half, k + 1)]).wait_recv()
                place = region(shifted(axis, -by * here), half)
                send(place, place, neighbour(axis, by), first + number[(way, half, k)])
            if j:
                yield j
            else:
                yield 0
            if j + 1 < len(order):
                for way, half, k in step:
                    if k == 1:
                        by = 1 if way == 0 else -1
                        place = region(shifted(axis, -by * (hops(n, way, half))), half)
                        remote(place, place, neighbour(axis, by), first + number[(way, half, 1)]).wait_recv()
        for way, half, k in order[-1]:
            by = 1 if way == 0 else -1
            place = region(shifted(axis, -by * hops(n, way, half)), half)
            remote(place, place, neighbour(axis, by), first + number[(way, half, 1)]).wait_recv()

    def reduce_scatter(axis, own_term, sbuf, rbuf, finish):
        n = RING[axis]
        order = ring_order(n)
        number, slot = {}, {}
        for step in order:
            for item in step:
                number[item] = len(number)
        for way in (0, 1):
            for i, item in enumerate([m for step in order for m in step if m[0] == way]):
                slot[item] = i
        first = sems(len(number))

        def arrival(item):
            way = item[0]
            place = rbuf.at[way, slot[item]]
            remote(sbuf.at[way, slot[item]], place, neighbour(axis, 1 if way == 0 else -1), first + number[item]).wait_recv()

        for j, step in enumerate(order):
            if j == 0:
                for item in step:
                    way, half, k = item
                    value = own_term(shifted(axis, (1 if way == 0 else -1) * k), half)
                    sbuf[way, slot[item]] = value.astype(BF16)
            for item in step:
                way, half, k = item
                by = 1 if way == 0 else -1
                if j == 0:
                    send(sbuf.at[way, slot[item]], rbuf.at[way, slot[item]], neighbour(axis, by), first + number[item])
                    continue
                value = own_term(shifted(axis, by * k), half)
                before = (way, half, k + 1)
                arrival(before)
                sbuf[way, slot[item]] = (value + rbuf[way, slot[before]].astype(F32)).astype(BF16)
                send(sbuf.at[way, slot[item]], rbuf.at[way, slot[item]], neighbour(axis, by), first + number[item])
            yield j
        for half in (0, 1):
            value = own_term(pos[axis], half)
            for way in (0, 1):
                arrival((way, half, 1))
                value = value + rbuf[way, slot[(way, half, 1)]].astype(F32)
            finish(half, value)

    def merged(part):
        name, base, rows, axis = part
        r = rows // NX
        prod, sbuf1, rbuf1, share, share16, rbuf2, whole = bufs[name]
        other = "y" if axis == "x" else "x"
        n2 = RING[other]

        loaded("dw" if base < FF_HERE else "ow", "enc")
        for j in range(0, BLOCKS, 2):
            out = dot(wv[base : base + rows], enc[:, j * LANES : (j + 2) * LANES])
            for i in (0, 1):
                prod[j + i] = out[:, i * LANES : (i + 1) * LANES].reshape(NX, r, LANES)

        def term_x(dest, half):
            return prod[half * (NY // 2) : (half + 1) * (NY // 2), dest]

        def term_y(dest, half):
            return prod[dest, half * (NX // 2) : (half + 1) * (NX // 2)]

        def keep(half, value):
            at = pl.ds(half * (n2 // 2), n2 // 2)
            share[at] = value
            share16[at] = value.astype(BF16)

        yield from reduce_scatter(axis, term_x if axis == "x" else term_y, sbuf1, rbuf1, keep)
        sem = sems(2)
        to_all(other, lambda by: share16.at[shifted(other, by)], lambda by: rbuf2.at[by - 1], sem)
        late.append((rbuf2, send_sem.at[sem]))
        yield "scattered"
        total = share[pos[other]]
        wait_bytes(rbuf2, recv_sem.at[sem])
        for i in range(n2 - 1):
            total = total + rbuf2[i].astype(F32)
        whole[y, x] = total.astype(BF16)
        to_all(other, lambda by: whole.at[y, x], lambda by: whole.at[y, x], sem + 1)
        late.append((rbuf2, send_sem.at[sem + 1]))
        yield "shared"
        wait_bytes(rbuf2, recv_sem.at[sem + 1])
        if axis == "x":
            yield from all_gather("x", lambda i, half: whole.at[pl.ds(half * (NY // 2), NY // 2), i])
        else:
            yield from all_gather("y", lambda i, half: whole.at[i, pl.ds(half * (NX // 2), NX // 2)])
        yield "done"

    def attend(row, h, diagonal):
        lanes = slice(h * HEAD, (h + 1) * HEAD)
        keys = kv[0, :, row].reshape(NX * ROWS, HEAD)
        values = kv[1, :, row].reshape(NX * ROWS, HEAD)
        s = nt_dot(qv[:, lanes], keys)
        if diagonal:
            at = lax.broadcasted_iota(jnp.int32, s.shape, 1)
            place = (lax.shift_right_logical(at, 7) & 3) * ROWS + lax.shift_right_logical(at, 9) * 128 + (at & 127)
            mine = x * ROWS + lax.broadcasted_iota(jnp.int32, s.shape, 0)
            s = jnp.where(place <= mine, s, F32(-1e30))
        new_top = jnp.max(s, axis=1, keepdims=True)
        if not diagonal:
            old_top = top[h][:, :1]
            new_top = jnp.maximum(old_top, new_top)
        weights = jnp.exp2((s - new_top) * F32(EXP_SCALE)).astype(BF16)
        extended = jnp.concatenate([values, jnp.ones_like(values)], axis=1)
        update = dot(weights, extended)
        if not diagonal:
            update = update + acc[h] * jnp.exp2((old_top - new_top) * F32(EXP_SCALE))
        acc[h] = update
        top[h] = jnp.broadcast_to(new_top, (ROWS, LANES))

    waiting = []

    def attention():
        loaded("q")
        for _ in range(NY * HEADS):
            while not waiting:
                step("k")
            row, h, diagonal = waiting.pop(0)
            if diagonal:
                attend(row, h, True)
            else:

                @pl.when(row < y)
                def _():
                    attend(row, h, False)

            yield "attended"
        for h in range(HEADS):
            state = acc[h]
            att[:, h * HEAD : (h + 1) * HEAD] = (state[:, :HEAD] / state[:, HEAD:]).astype(BF16)
        store(att, att_out)

    def keys_and_values():
        loaded("k", "v")
        gather = all_gather("y", lambda i, half: kv.at[half, core, i, x])

        def spread(row):
            ring = all_gather("x", lambda i, half: kv.at[half, core, row, i])
            next(ring)
            return ring

        def hand_over(row):
            first = sems(2)
            for half in (0, 1):
                place = kv.at[half, core, row]
                send(place, place, {"tp": sibling}, first + half)
            return first

        def handed(row, first):
            for half in (0, 1):
                place = kv.at[half, 1 - core, row]
                remote(place, place, {"tp": sibling}, first + half).wait_recv()

        def arrived(rings):
            for ring in rings:
                for _ in ring:
                    pass

        next(gather)
        before = [spread(y)]
        at = [y]
        yield "sent"
        for k in range(1, NY // 2 + 2):
            rings, rows = [], []
            if k < NY // 2:
                next(gather)
                rows = [shifted("y", -k), shifted("y", k)]
            elif k == NY // 2:
                for _ in gather:
                    pass
                rows = [shifted("y", k)]
            rings = [spread(row) for row in rows]
            for ring in before:
                next(ring)
            yield "sent"
            arrived(before)
            firsts = [hand_over(row) for row in at]
            yield "handed over"
            for row, first in zip(at, firsts):
                handed(row, first)
                waiting.extend((row, h, k == 1) for h in range(HEADS))
            yield "here"
            before, at = rings, rows

    half_tokens = ROWS // 2

    def exchange(group, sem):
        part, from_core, half, recv, full = group

        def z_device(o):
            return {"tp": lax.rem(zi + o, NT // 2) * 2 + core}

        theirs = pl.ds(pl.multiple_of((1 - core) * half_tokens, half_tokens), half_tokens)
        ours = pl.ds(pl.multiple_of(core * half_tokens, half_tokens), half_tokens)

        def to_core():
            return pltpu.make_async_remote_copy(
                src_ref=part.at[theirs],
                dst_ref=from_core,
                send_sem=z_send.at[sem],
                recv_sem=z_recv.at[sem],
                device_id={"tp": sibling},
                device_id_type=MESH,
            )

        to_core().start()
        yield "given"
        to_core().wait_recv()
        half[...] = (part[ours].astype(F32) + from_core[...].astype(F32)).astype(BF16)

        def give(o):
            to = lax.rem(zi + o, NT // 2)
            pltpu.make_async_remote_copy(
                src_ref=half.at[pl.ds(pl.multiple_of(to * SLICE, SLICE), SLICE)],
                dst_ref=recv.at[o - 1],
                send_sem=z_send.at[sem + 1],
                recv_sem=z_recv.at[sem + 1],
                device_id=z_device(o),
                device_id_type=MESH,
            ).start()

        for o in farthest_first(NT // 2):
            give(o)
        yield "scattered"
        total = half[pl.ds(pl.multiple_of(zi * SLICE, SLICE), SLICE)].astype(F32)
        wait_bytes(recv, z_recv.at[sem + 1])
        for o in range(NT // 2 - 1):
            total = total + recv[o].astype(F32)
        mine = pl.ds(pl.multiple_of(core * half_tokens + zi * SLICE, SLICE), SLICE)
        full[mine] = total.astype(BF16)

        def share(o):
            pltpu.make_async_remote_copy(
                src_ref=full.at[mine],
                dst_ref=full.at[mine],
                send_sem=z_send.at[sem + 2],
                recv_sem=z_recv.at[sem + 2],
                device_id=z_device(o),
                device_id_type=MESH,
            ).start()

        for o in farthest_first(NT // 2):
            share(o)
        yield "shared"
        wait_bytes(recv, z_recv.at[sem + 2])

        def whole_half(rows):
            return pltpu.make_async_remote_copy(
                src_ref=full.at[rows],
                dst_ref=full.at[rows],
                send_sem=z_send.at[sem + 3],
                recv_sem=z_recv.at[sem + 3],
                device_id={"tp": sibling},
                device_id_type=MESH,
            )

        whole_half(ours).start()
        yield "handed over"
        whole_half(theirs).wait_recv()
        yield "done"
        to_core().wait_send()
        wait_bytes(recv, z_send.at[sem + 1])
        wait_bytes(recv, z_send.at[sem + 2])
        whole_half(ours).wait_send()

    def exchange_straight(group, sem):
        part, recv, full = group
        mine = pl.ds(pl.multiple_of(tp * SLICE, SLICE), SLICE)

        def to_each(src, dst, at):
            for apart in farthest_first(NT // 2):
                for other in (0, 1):
                    one(apart, other, src, dst, at)
            one(0, 1, src, dst, at)

        def one(apart, other, src, dst, at):
            z = lax.rem(zi + apart, NT // 2)
            to = z * 2 + (core if other == 0 else 1 - core)
            pltpu.make_async_remote_copy(
                src_ref=src(to),
                dst_ref=dst(2 * apart + other - 1),
                send_sem=z_send.at[sem + at],
                recv_sem=z_recv.at[sem + at],
                device_id={"tp": to},
                device_id_type=MESH,
            ).start()

        to_each(lambda to: part.at[pl.ds(pl.multiple_of(to * SLICE, SLICE), SLICE)], lambda slot: recv.at[slot], 0)
        yield "scattered"
        total = part[mine].astype(F32)
        wait_bytes(recv, z_recv.at[sem])
        for o in range(NT - 1):
            total = total + recv[o].astype(F32)
        full[mine] = total.astype(BF16)
        to_each(lambda to: full.at[mine], lambda slot: full.at[mine], 1)
        yield "shared"
        wait_bytes(recv, z_recv.at[sem + 1])
        yield "done"
        for at in (0, 1):
            wait_bytes(recv, z_send.at[sem + at])

    outs = []

    def store(src, dst):
        copy = pltpu.make_async_copy(src, dst, local_sem.at[len(loads) + len(outs)])
        copy.start()
        outs.append(copy)

    whole = {name: bufs[name][6] for name, *_ in PARTS}
    rows_of = {name: rows for name, _, rows, _ in PARTS}

    def block(name, j):
        return whole[name][j].reshape(rows_of[name], LANES)

    def grad_code():
        loaded("cot", "dec")
        grad_refs[0][...] = nt_dot(cot[...], dec[...]).astype(BF16)
        yield from exchange(grad_refs, 0)

    def code(g):
        loaded("hid")
        for name in "uac":
            finish(name)
        reach("b", READY[g])
        for i, by in enumerate(GROUPS[g]):
            j = shifted("y", by)
            total = dot(hid[:, :SPLIT], block("a", j)) + dot(hid[:, SPLIT:], block("b", j)) + dot(att[...], block("c", j))
            code_refs[g][0][:, i * LANES : (i + 1) * LANES] = total.astype(BF16)
        if g == len(GROUPS) - 1:
            yield from exchange_straight(code_refs[g], 4 + 4 * g)
        else:
            yield from exchange(code_refs[g], 4 + 4 * g)

    def back(name):
        total = None
        for j in range(0, BLOCKS, 2):
            pair = jnp.concatenate([block(name, j), block(name, j + 1)], axis=1)
            term = nt_dot(grad_refs[4][:, LANES * j : LANES * (j + 2)], pair)
            total = term if total is None else total + term
        return total.astype(BF16)

    def gradients():
        finish("g")
        finish("a")
        gh[:, :SPLIT] = back("a")
        yield "first"
        finish("b")
        gh[:, SPLIT:] = back("b")
        store(gh, gh_out)
        yield "second"
        finish("c")
        ga[...] = back("c")
        store(ga, ga_out)
        yield "third"

    gens = {part[0]: merged(part) for part in PARTS}
    gens.update(k=keys_and_values(), u=attention(), g=grad_code(), m=gradients())
    gens.update({str(g): code(g) for g in range(len(GROUPS))})
    taken = {name: 0 for name in gens}
    ended = set()

    def sent():
        for copy in started:
            copy.wait_send()
        started.clear()
        for ref, sem in late:
            wait_bytes(ref, sem)
        late.clear()

    def step(name):
        taken[name] += 1
        if name not in ended and next(gens[name], None) is None:
            ended.add(name)
        if name == str(len(GROUPS) - 1) and taken[name] == 2:
            sent()

    def finish(name):
        while name not in ended:
            step(name)

    def reach(name, count):
        while taken[name] < count and name not in ended:
            step(name)

    pl.semaphore_wait(barrier, NX - 1 + NY - 1 + NT - 1)
    for name in "".join(ORDER):
        step(name)
    result = None
    for g, cols in enumerate(GROUPS):
        reach(str(g), 5)
        for i, by in enumerate(cols):
            rows = pl.ds(pl.multiple_of(shifted("y", by) * LANES, LANES), LANES)
            term = dot(code_refs[g][-1][:, i * LANES : (i + 1) * LANES], dec[rows])
            result = term if result is None else result + term
    decd[...] = result.astype(BF16)
    store(decd, dec_out)
    for name in gens:
        finish(name)
    sent()
    for copy in outs:
        copy.wait()


def deliver(*refs):
    ins, outs, held, sems = refs[:4], refs[4:8], refs[8:12], refs[12]
    loads = [pltpu.make_async_copy(ins[i], held[i], sems.at[i]) for i in range(4)]
    stores = [pltpu.make_async_copy(held[i], outs[i], sems.at[4 + i]) for i in range(4)]
    for copy in loads:
        copy.start()
    for copy, then in zip(loads, stores):
        copy.wait()
        then.start()
    for copy in stores:
        copy.wait()


def per_device(*args):
    anywhere = pl.BlockSpec(memory_space=pl.ANY)
    scratch = [
        pltpu.VMEM((ROWS, ATT_HERE), BF16),
        pltpu.VMEM((ROWS, FF_HERE), BF16),
        pltpu.VMEM((FF_HERE + ATT_HERE, 256), BF16),
        pltpu.VMEM((256, R), BF16),
        pltpu.VMEM((R, 512), BF16),
        pltpu.VMEM((ROWS, 512), BF16),
        pltpu.VMEM((2, 2, NY, NX, 128, HEAD), BF16),
        pltpu.VMEM((HEADS, ROWS, 2 * HEAD), F32),
        pltpu.VMEM((HEADS, ROWS, LANES), F32),
        pltpu.VMEM((ROWS, ATT_HERE), BF16),
        pltpu.VMEM((ROWS, 512), BF16),
        pltpu.VMEM((ROWS, FF_HERE), BF16),
        pltpu.VMEM((ROWS, ATT_HERE), BF16),
    ]
    for width in (R, *(LANES * len(cols) for cols in GROUPS[:-1])):
        scratch += [
            pltpu.VMEM((ROWS, width), BF16),
            pltpu.VMEM((ROWS // 2, width), BF16),
            pltpu.VMEM((ROWS // 2, width), BF16),
            pltpu.VMEM((NT // 2 - 1, SLICE, width), BF16),
            pltpu.VMEM((ROWS, width), BF16),
        ]
    width = LANES * len(GROUPS[-1])
    scratch += [pltpu.VMEM((ROWS, width), BF16), pltpu.VMEM((NT - 1, SLICE, width), BF16), pltpu.VMEM((ROWS, width), BF16)]
    for part in PARTS:
        scratch += scratch_of(part)
    scratch += [
        pltpu.SemaphoreType.DMA((SEMS,)),
        pltpu.SemaphoreType.DMA((SEMS,)),
        pltpu.SemaphoreType.DMA((4 + 4 * len(GROUPS),)),
        pltpu.SemaphoreType.DMA((4 + 4 * len(GROUPS),)),
        pltpu.SemaphoreType.DMA((LOCAL,)),
    ]
    shapes = (
        jax.ShapeDtypeStruct((ROWS, ATT_HERE), BF16),
        jax.ShapeDtypeStruct((ROWS, 512), BF16),
        jax.ShapeDtypeStruct((ROWS, FF_HERE), BF16),
        jax.ShapeDtypeStruct((ROWS, ATT_HERE), BF16),
    )
    results = pl.pallas_call(
        kernel,
        out_shape=shapes,
        in_specs=[anywhere] * 9,
        out_specs=(anywhere,) * 4,
        scratch_shapes=scratch,
        compiler_params=pltpu.CompilerParams(
            collective_id=0, has_side_effects=True, vmem_limit_bytes=56 * 1024 * 1024
        ),
    )(*args)
    return pl.pallas_call(
        deliver,
        out_shape=shapes,
        in_specs=[anywhere] * 4,
        out_specs=(anywhere,) * 4,
        scratch_shapes=[pltpu.VMEM(shape.shape, BF16) for shape in shapes] + [pltpu.SemaphoreType.DMA((8,))],
        compiler_params=pltpu.CompilerParams(vmem_limit_bytes=60 * 1024 * 1024),
    )(*results)


def solution(mesh):
    return jax.shard_map(
        per_device,
        mesh=mesh,
        in_specs=(
            P("ctx", "tp"),
            P("ctx", None),
            P("ctx", None),
            P("ctx", "tp"),
            P("tp", "ctx"),
            P("tp", "ctx"),
            P("ctx", None),
            P(None, "tp"),
            P("ctx", "tp"),
        ),
        out_specs=(P("ctx", "tp"), P("ctx", "tp"), P("ctx", "tp"), P("ctx", "tp")),
        check_vma=False,
    )
```
